32 devices in a mesh: parts: 2 (over y), occ: 8 (over z, core), aux: 2 (over x).
Axes of the slice: x: 2, y: 2, z: 4, core: 2. Of those that a mesh axis runs over, the one named last changes fastest.
Arguments:
- raw_ints: bfloat16 [32, 256, 512], P('parts', 'aux', 'occ'), parts along dimension 0, may hold values from -0.375 to 0.375
- kept: int32 [16, 4, 4], P('parts'), parts along dimension 0, may hold values from 0 to 128
- eps_occ: bfloat16 [32], P(('parts', 'occ')), parts along dimension 0, may hold values from -1.1953125 to -0.3984375
- eps_vir: bfloat16 [512], P('parts'), parts along dimension 0, may hold values from 0.29882812 to 3
- metric_factor: bfloat16 [512, 512], replicated, may hold values from -0.25 to 0.25
Outputs:
- pair_energy: float32 [32, 16], P(('parts', 'occ'), 'aux'), parts along dimension 0
The draws below stay inside these ranges and needn't reach their ends.
There are 2 independent parts, one for each index of `parts`. The reference program is written for one: setup_inputs(seed, part) draws one part's arguments, and reference() takes and returns one part's arrays. A program takes and returns all parts, laid end to end along the dimension named above; an argument that names none is the same for every part. Nothing has to cross between parts.
All inputs are finite; a program needn't handle non-finite values.
Results may differ from the reference program's by a relative error of at most 0.0003.
Values may be sent and summed in bfloat16 or wider, within the bound.
A program may use at most 64 MiB of HBM per device.

```python
import math
import jax
import jax.numpy as jnp
from jax import lax

OCC_DEV = 2
VB = 64
PB = 128
NVB = 4
NPB = 4
V = 256
NAUX = 512
NOCC = 16
N_OCC = 8


def with_ends(drawn, key, least, high):
    longest = drawn.shape.index(max(drawn.shape))
    spots = []
    for shift in (0, 1):
        where = [jax.random.randint(jax.random.fold_in(key, axis), (), 0, length) for axis, length in enumerate(drawn.shape)]
        where[longest] = (where[longest] + shift) % drawn.shape[longest]
        spots.append(tuple(where))
    return drawn.at[spots[0]].set(least).at[spots[1]].set(high)


def shard_levels(rng, extent, pieces, low, largest):
    level = 1.0
    for position, shards_of in pieces:
        draws = jax.random.uniform(jax.random.fold_in(jax.random.fold_in(rng, 6), position), (shards_of,), jnp.float32, low / len(pieces), largest / len(pieces))
        level = level * jnp.repeat(jnp.exp(draws), extent[position] // shards_of).reshape((-1,) + (1,) * (len(extent) - 1 - position))
    return level


def gaussian(key, extent, scale, reach, pieces=(), kind=jnp.bfloat16):
    loudness = shard_levels(key, extent, pieces, -0.22, 0.18) if pieces else 1.0
    array = jax.random.normal(key, extent, jnp.float32) * scale * loudness
    return jnp.minimum(jnp.maximum(array, -reach), reach).astype(kind)


def setup_inputs(seed: int = 0, part: int = 0) -> dict:
    seeds = jax.random.split(jax.random.key(seed), 6)
    part_splits = jax.random.split(jax.random.fold_in(seeds[5], part), 6)
    return {
        "raw_ints": gaussian(part_splits[0], (NOCC, V, NAUX), (2.0 * (NAUX * V * V) ** -0.25), 0.375, ((1, 2), (2, 8))),
        "kept": with_ends(jax.random.randint(part_splits[1], (N_OCC, NVB, NPB), 0, PB + 1), jax.random.fold_in(part_splits[1], 1), 0, PB).astype(jnp.int32),
        "eps_occ": jnp.clip(-1.1953125 + 0.796875 * jax.random.uniform(part_splits[2], (NOCC,), jnp.float32) ** shard_levels(part_splits[2], (NOCC,), ((0, 8),), -0.2, 0.2), -1.1953125, -0.3984375).astype(jnp.bfloat16),
        "eps_vir": jnp.clip(jnp.exp(jax.random.uniform(part_splits[3], (V,), jnp.float32, math.log(0.29882812), math.log(3.0))), 0.29882812, 3.0).astype(jnp.bfloat16),
        "metric_factor": gaussian(seeds[4], (NAUX, NAUX), NAUX ** -0.5, 0.25),
    }


def reference(raw_ints, kept, eps_occ, eps_vir, metric_factor):
    expanded = jnp.repeat(jnp.repeat(jnp.repeat(kept, OCC_DEV, axis=0), VB, axis=1), PB, axis=2)
    offset = jnp.arange(NAUX, dtype=jnp.int32) % PB
    screened = jnp.where(offset[None, None, :] < expanded, raw_ints, jnp.zeros_like(raw_ints))
    factors = jnp.dot(screened.reshape(NOCC * V, NAUX), metric_factor, preferred_element_type=jnp.float32)
    factors = factors.astype(jnp.bfloat16).reshape(NOCC, V, NAUX).astype(jnp.float32)
    occ_levels = eps_occ.astype(jnp.float32)
    vir_levels = eps_vir.astype(jnp.float32)

    def one_row(packed):
        own_factor, own_level = packed
        direct = jnp.einsum("ap,jbp->ajb", own_factor, factors, precision=lax.Precision.HIGHEST)
        swapped = jnp.einsum("bp,jap->ajb", own_factor, factors, precision=lax.Precision.HIGHEST)
        denom = vir_levels[:, None, None] + vir_levels[None, None, :] - own_level - occ_levels[None, :, None]
        return -jnp.sum(direct * (2.0 * direct - swapped) / denom, axis=(0, 2))

    return lax.map(one_row, (factors, occ_levels))
```

```python
import functools

import jax
import jax.numpy as jnp
from jax import lax
from jax.experimental import pallas as pl
from jax.experimental.pallas import tpu as pltpu
from jax.sharding import PartitionSpec as P

VB = 64
PB = 128
MESH = pl.DeviceIdType.MESH
F32 = jnp.float32


def needs(x, z):
    first = jnp.maximum(z - 1, 0)
    second = jnp.where(z == 0, 1, jnp.where(z == 3, 3, 2 + x))
    return first, second


def kernel(
    raw_ref, kept_ref, occ_ref, row_ref, col_ref, metric_ref, out_ref,
    blocks, mat, fac, base, levels, energy, shares,
    recv, s_right, s_left, s_aux, s_core, s_lev, r_lev, s_out, r_out,
):
    occ = lax.axis_index("occ")
    x = lax.axis_index("aux")
    z, c = occ // 2, occ % 2
    me = occ * 2 + x
    left_lim = jnp.where(z == 1, 2, 4)
    left_lim_in = jnp.where(z == 0, 2, 4)
    own = needs(x, z)
    other = needs(1 - x, z)

    barrier = pltpu.get_barrier_semaphore()
    for d in range(1, 16):
        peer = (me + d) % 16
        pl.semaphore_signal(
            barrier, inc=1, device_id={"occ": peer // 2, "aux": peer % 2}, device_id_type=MESH
        )

    lane = lax.broadcasted_iota(jnp.int32, (2 * VB, 2 * VB), 1) % VB + c * VB
    row = lax.broadcasted_iota(jnp.int32, (2 * VB, 2 * VB), 0)
    for k in range(8):
        both = jnp.concatenate([raw_ref[2 * k], raw_ref[2 * k + 1]], axis=1).astype(F32)
        limit = jnp.where(row < VB, kept_ref[k, 2 * x, z], kept_ref[k, 2 * x + 1, z])
        blocks[z, x, c, k // 2, k % 2] = jnp.where(lane < limit, both, 0.0).astype(jnp.bfloat16)
    levels[occ] = occ_ref[...]

    pl.semaphore_wait(barrier, 15)

    def copy(zs, xs, cs, n, send_sem, to_occ, to_x):
        return pltpu.make_async_remote_copy(
            src_ref=blocks.at[zs, xs, cs, n],
            dst_ref=blocks.at[zs, xs, cs, n],
            send_sem=send_sem,
            recv_sem=recv.at[zs, xs, cs, n],
            device_id={"occ": to_occ, "aux": to_x},
            device_id_type=MESH,
        )

    right_id = jnp.minimum(occ + 2, 7)
    left_id = jnp.maximum(occ - 2, 0)
    core_id = 2 * z + 1 - c

    def go_right(zs, n):
        return copy(zs, x, c, n, s_right.at[zs, n], right_id, x)

    def go_left(zs, n):
        return copy(zs, x, c, n, s_left.at[zs, n], left_id, x)

    def go_aux(zs, m):
        return copy(zs, x, c, other[m], s_aux.at[zs, m], occ, 1 - x)

    def go_core(zs, xs, m):
        return copy(zs, xs, c, own[m], s_core.at[zs, xs, m], core_id, x)

    def arrived(zs, xs, cs, n):
        copy(zs, xs, cs, n, s_right.at[0, 0], core_id, x).wait_recv()

    def spread(zs):
        for m in range(2):
            go_aux(zs, m).start()
        for m in range(2):
            go_core(zs, x, m).start()

    def take_aux(zs):
        for m in range(2):
            arrived(zs, 1 - x, c, own[m])
            go_core(zs, 1 - x, m).start()

    for n in range(4):
        @pl.when((z < 3) & (n >= z))
        def _():
            go_right(z, n).start()

        @pl.when((z > 0) & (n < left_lim))
        def _():
            go_left(z, n).start()
    spread(z)

    def level_copy(d):
        to = (occ + d) % 8
        return pltpu.make_async_remote_copy(
            src_ref=levels.at[occ], dst_ref=levels.at[occ],
            send_sem=s_lev.at[d], recv_sem=r_lev.at[d],
            device_id={"occ": to}, device_id_type=MESH,
        )

    def level_wait(d):
        frm = (occ + 8 - d) % 8
        pltpu.make_async_remote_copy(
            src_ref=levels.at[frm], dst_ref=levels.at[frm],
            send_sem=s_lev.at[d], recv_sem=r_lev.at[d],
            device_id={"occ": (occ + d) % 8}, device_id_type=MESH,
        ).wait_recv()

    for d in range(1, 8):
        level_copy(d).start()
    base[...] = col_ref[...] + row_ref[...]
    energy[...] = jnp.zeros_like(energy)

    for t in range(1, 4):
        @pl.when(z >= t)
        def _():
            zs = jnp.maximum(z - t, 0)
            for n in range(4):
                @pl.when(n >= z - 1)
                def _():
                    arrived(zs, x, c, n)

                @pl.when((z < 3) & (n >= z))
                def _():
                    go_right(zs, n).start()

        @pl.when(z + t <= 3)
        def _():
            zs = jnp.minimum(z + t, 3)
            for n in range(4):
                @pl.when(n < left_lim_in)
                def _():
                    arrived(zs, x, c, n)

                @pl.when((z > 0) & (n < left_lim))
                def _():
                    go_left(zs, n).start()

        @pl.when(z >= t)
        def _():
            spread(jnp.maximum(z - t, 0))

        @pl.when(z + t <= 3)
        def _():
            spread(jnp.minimum(z + t, 3))

        if t == 1:
            take_aux(z)
        else:
            @pl.when(z >= t - 1)
            def _():
                take_aux(jnp.maximum(z - t + 1, 0))

            @pl.when(z + t - 1 <= 3)
            def _():
                take_aux(jnp.minimum(z + t - 1, 3))

    @pl.when(z >= 3)
    def _():
        take_aux(jnp.maximum(z - 3, 0))

    @pl.when(z + 3 <= 3)
    def _():
        take_aux(jnp.minimum(z + 3, 3))

    for zs in range(4):
        for xs in range(2):
            for m in range(2):
                arrived(zs, xs, 1 - c, own[m])

    diag = (x == 0) & ((z == 0) | (z == 3))
    for kk in range(4):
        @pl.when((diag & (kk // 2 == c)) | (jnp.logical_not(diag) & ((kk == c) | (kk >= 2))))
        def _():
            n = own[kk // 2]
            for xs in range(2):
                for zs in range(4):
                    t0 = blocks[zs, xs, 0, n, kk % 2]
                    t1 = blocks[zs, xs, 1, n, kk % 2]
                    mat[pl.ds(xs * 128, 128), pl.ds(zs * 128, 128)] = jnp.concatenate(
                        [t0[:, :VB], t1[:, :VB]], axis=1)
                    mat[pl.ds(256 + xs * 128, 128), pl.ds(zs * 128, 128)] = jnp.concatenate(
                        [t0[:, VB:], t1[:, VB:]], axis=1)
            prod = jnp.dot(mat[...], metric_ref[...], preferred_element_type=F32)
            prod = prod.astype(jnp.bfloat16)
            fac[2 * kk] = prod[:256]
            fac[2 * kk + 1] = prod[256:]

    for d in range(1, 8):
        level_wait(d)

    rows8 = lax.broadcasted_iota(jnp.int32, (8, 128), 0)
    lanes8 = lax.broadcasted_iota(jnp.int32, (8, 128), 1)

    def one_pair(t, carry):
        li = jnp.where(diag, 4 * c + t % 4, 2 * c + t // 4)
        lj = jnp.where(diag, 4 * c + (t % 4 + t // 4) % 4, 4 + t % 4)
        gi = 4 * jnp.where(li < 4, own[0], own[1]) + li % 4
        gj = 4 * jnp.where(lj < 4, own[0], own[1]) + lj % 4
        fi, fj = fac[li], fac[lj]
        dims = (((1,), (1,)), ((), ()))
        direct = lax.dot_general(fi, fj, dims, preferred_element_type=F32)
        swapped = lax.dot_general(fj, fi, dims, preferred_element_type=F32)
        pair_level = levels[gi // 2, pl.ds(gi % 2, 1), :] + levels[gj // 2, pl.ds(gj % 2, 1), :]
        pair_level = jnp.concatenate([pair_level, pair_level], axis=1)
        term = direct * (2.0 * direct - swapped) / (base[...] - pair_level)
        term = -jnp.sum(jnp.sum(term, axis=0, keepdims=True), axis=1, keepdims=True)
        energy[gi // 2] += jnp.where((rows8 == gi % 2) & (lanes8 == gj), term, 0.0)
        turned = (rows8 == gj % 2) & (lanes8 == gi) & (gi != gj)
        energy[gj // 2] += jnp.where(turned, term, 0.0)
        return carry

    lax.fori_loop(0, jnp.where(diag, 10, 8), one_pair, 0)

    def out_copy(d):
        to = (me + d) % 16
        return pltpu.make_async_remote_copy(
            src_ref=energy.at[to // 2], dst_ref=shares.at[d],
            send_sem=s_out.at[d], recv_sem=r_out.at[d],
            device_id={"occ": to // 2, "aux": to % 2}, device_id_type=MESH,
        )

    for d in range(1, 16):
        out_copy(d).start()

    for n in range(4):
        for t in range(4):
            @pl.when((z >= t) & (z < 3) & (n >= z))
            def _():
                go_right(jnp.maximum(z - t, 0), n).wait_send()

            @pl.when((z + t <= 3) & (z > 0) & (n < left_lim))
            def _():
                go_left(jnp.minimum(z + t, 3), n).wait_send()
    for zs in range(4):
        for m in range(2):
            go_aux(zs, m).wait_send()
            for xs in range(2):
                go_core(zs, xs, m).wait_send()
    for d in range(1, 8):
        level_copy(d).wait_send()

    total = energy[occ]
    for d in range(1, 16):
        out_copy(d).wait_recv()
        total = total + shares[d]
    out_ref[...] = jnp.where(x == 0, total[0:2, 0:8], total[0:2, 8:16])
    for d in range(1, 16):
        out_copy(d).wait_send()


def fused_body(raw_ints, kept, eps_occ, eps_vir, metric_factor):
    bf, dma = jnp.bfloat16, pltpu.SemaphoreType.DMA
    vir = eps_vir.astype(F32)
    occ_tile = jnp.broadcast_to(jnp.tile(eps_occ.astype(F32), 4)[:, None], (8, 128))
    vmem = pl.BlockSpec(memory_space=pltpu.VMEM)
    return pl.pallas_call(
        kernel,
        out_shape=jax.ShapeDtypeStruct((2, 8), F32),
        in_specs=[vmem, pl.BlockSpec(memory_space=pltpu.SMEM), vmem, vmem, vmem, vmem],
        out_specs=vmem,
        scratch_shapes=[
            pltpu.VMEM((4, 2, 2, 4, 2, 128, 128), bf),
            pltpu.VMEM((512, 512), bf),
            pltpu.VMEM((8, 256, 512), bf),
            pltpu.VMEM((256, 256), F32),
            pltpu.VMEM((8, 8, 128), F32),
            pltpu.VMEM((8, 8, 128), F32),
            pltpu.VMEM((16, 8, 128), F32),
            dma((4, 2, 2, 4)),
            dma((4, 4)),
            dma((4, 4)),
            dma((4, 2)),
            dma((4, 2, 2)),
            dma((8,)),
            dma((8,)),
            dma((16,)),
            dma((16,)),
        ],
        compiler_params=pltpu.CompilerParams(
            collective_id=0, has_side_effects=True, vmem_limit_bytes=40 * 2**20
        ),
    )(raw_ints, kept, occ_tile, vir[None, :], vir[:, None], metric_factor)


def pair_terms(
    left_slice, right_all, left_cols, right_slice, own_levels, part_levels, vir_rows, vir_cols
):
    direct = jnp.einsum("iap,jbp->iajb", left_slice, right_all, preferred_element_type=jnp.float32)
    swapped = jnp.einsum(
        "ibp,jap->iajb", left_cols, right_slice, preferred_element_type=jnp.float32
    )
    own_f = own_levels.astype(jnp.float32)
    part_f = part_levels.astype(jnp.float32)
    rows_f = vir_rows.astype(jnp.float32)
    cols_f = vir_cols.astype(jnp.float32)
    denom = (
        rows_f[None, :, None, None]
        + cols_f[None, None, None, :]
        - own_f[:, None, None, None]
        - part_f[None, None, :, None]
    )
    return -jnp.sum(direct * (2.0 * direct - swapped) / denom, axis=(1, 3))


def body(raw_ints, kept, eps_occ, eps_vir, metric_factor):
    total_occ = raw_ints.shape[0]
    slice_vir = raw_ints.shape[1]
    slice_aux = raw_ints.shape[2]
    naux_all = metric_factor.shape[0]
    own_occ = eps_occ.shape[0]
    block_count = kept.shape[2]
    occ_index = lax.axis_index("occ")
    aux_index = lax.axis_index("aux")
    repeated = jnp.repeat(jnp.repeat(kept, total_occ // kept.shape[0], axis=0), VB, axis=1)
    kept_vir = lax.dynamic_slice_in_dim(repeated, aux_index * slice_vir, slice_vir, 1)
    aux_start = occ_index * slice_aux
    positions = aux_start + jnp.arange(slice_aux, dtype=jnp.int32)
    block_ids = positions // PB
    onehot = (block_ids[:, None] == jnp.arange(block_count, dtype=jnp.int32)[None, :]).astype(
        jnp.int32
    )
    kept_here = jnp.sum(kept_vir[:, :, None, :] * onehot[None, None, :, :], axis=3)
    offset = positions % PB
    screened = jnp.where(offset[None, None, :] < kept_here, raw_ints, jnp.zeros_like(raw_ints))
    relaid = lax.all_to_all(screened, "occ", split_axis=0, concat_axis=2, tiled=True)
    own_slice = jnp.dot(
        relaid.reshape(own_occ * slice_vir, naux_all),
        metric_factor,
        preferred_element_type=jnp.float32,
    )
    own_slice = own_slice.astype(jnp.bfloat16).reshape(own_occ, slice_vir, naux_all)
    vir_rows = lax.dynamic_slice_in_dim(eps_vir, aux_index * slice_vir, slice_vir)
    empty = jnp.zeros((own_occ, total_occ), jnp.float32)
    own_full = lax.all_gather(own_slice, "aux", axis=1, tiled=True)
    partner_rows = lax.all_gather(own_full, "occ", axis=0, tiled=True)
    partner_levels = lax.all_gather(eps_occ, "occ", axis=0, tiled=True)
    blocks_in = partner_rows.shape[0] // own_occ

    def add_block(block_no, totals):
        part_block = lax.dynamic_slice_in_dim(partner_rows, block_no * own_occ, own_occ, 0)
        part_level = lax.dynamic_slice_in_dim(partner_levels, block_no * own_occ, own_occ, 0)
        part_slice = lax.dynamic_slice_in_dim(part_block, aux_index * slice_vir, slice_vir, 1)
        term = pair_terms(
            own_slice, part_block, own_full, part_slice, eps_occ, part_level, vir_rows, eps_vir
        )
        column = block_no * own_occ
        before = lax.dynamic_slice_in_dim(totals, column, own_occ, 1)
        return lax.dynamic_update_slice_in_dim(totals, before + term, column, 1)

    energies = lax.fori_loop(0, blocks_in, add_block, empty)
    return lax.psum_scatter(energies, "aux", scatter_dimension=1, tiled=True)


def solution(mesh):
    in_specs = (
        P("parts", "aux", "occ"),
        P("parts", None, None),
        P(("parts", "occ")),
        P("parts"),
        P(),
    )
    out_specs = P(("parts", "occ"), "aux")
    fits = mesh.shape["occ"] == 8 and mesh.shape["aux"] == 2

    def step(raw_ints, kept, eps_occ, eps_vir, metric_factor):
        sizes = (raw_ints.shape, kept.shape, eps_occ.shape, eps_vir.shape)
        fused = fits and sizes == ((16, 128, 64), (8, 4, 4), (2,), (256,))
        run = fused_body if fused else body
        return run(raw_ints, kept, eps_occ, eps_vir, metric_factor)

    return jax.shard_map(step, mesh=mesh, in_specs=in_specs, out_specs=out_specs, check_vma=False)
```

```python
import jax
import jax.numpy as jnp
from jax import lax
from jax.experimental import pallas as pl
from jax.experimental.pallas import tpu as pltpu
from jax.sharding import PartitionSpec as P

VB = 64
PB = 128
MESH = pl.DeviceIdType.MESH
F32 = jnp.float32


def needs(x, z):
    first = jnp.maximum(z - 1, 0)
    second = jnp.where(z == 0, 1, jnp.where(z == 3, 3, 2 + x))
    return first, second


def kernel(
    raw_ref, kept_ref, occ_ref, vir_ref, metric_ref, out_ref,
    blocks, mat, fac, base, levels, energy, shares, gathered,
    recv, s_right, s_left, s_aux, s_core, s_lev, r_lev, s_out, r_out,
):
    occ = lax.axis_index("occ")
    x = lax.axis_index("aux")
    z, c = occ // 2, occ % 2
    me = occ * 2 + x
    left_lim = jnp.where(z == 1, 2, 4)
    left_lim_in = jnp.where(z == 0, 2, 4)
    own = needs(x, z)
    other = needs(1 - x, z)

    barrier = pltpu.get_barrier_semaphore()
    for d in range(1, 16):
        peer = (me + d) % 16
        pl.semaphore_signal(
            barrier, inc=1, device_id={"occ": peer // 2, "aux": peer % 2}, device_id_type=MESH
        )

    place = lax.broadcasted_iota(jnp.int32, (VB, 2 * VB), 0) + c * VB
    lane = lax.broadcasted_iota(jnp.int32, (VB, 2 * VB), 1)
    for k in range(8):
        limit = jnp.where(lane < VB, kept_ref[2 * x, z, k], kept_ref[2 * x + 1, z, k])
        for i in (2 * k, 2 * k + 1):
            kept_part = jnp.where(place < limit, raw_ref[i].astype(F32), 0.0)
            blocks[z, x, c, i // 4, i % 4] = kept_part.astype(jnp.bfloat16)
    pair = occ_ref[...].astype(F32)
    row8 = lax.broadcasted_iota(jnp.int32, (8, 128), 0)
    levels[occ] = jnp.where(row8 == 0, pair[:, 0:1], pair[:, 1:2])

    pl.semaphore_wait(barrier, 15)

    def copy(zs, xs, cs, n, send_sem, to_occ, to_x):
        return pltpu.make_async_remote_copy(
            src_ref=blocks.at[zs, xs, cs, n],
            dst_ref=blocks.at[zs, xs, cs, n],
            send_sem=send_sem,
            recv_sem=recv.at[zs, xs, cs, n],
            device_id={"occ": to_occ, "aux": to_x},
            device_id_type=MESH,
        )

    right_id = jnp.minimum(occ + 2, 7)
    left_id = jnp.maximum(occ - 2, 0)
    core_id = 2 * z + 1 - c

    def go_right(zs, n):
        return copy(zs, x, c, n, s_right.at[zs, n], right_id, x)

    def go_left(zs, n):
        return copy(zs, x, c, n, s_left.at[zs, n], left_id, x)

    def go_aux(zs, m):
        return copy(zs, x, c, other[m], s_aux.at[zs, m], occ, 1 - x)

    def go_core(zs, xs, m):
        return copy(zs, xs, c, own[m], s_core.at[zs, xs, m], core_id, x)

    def arrived(zs, xs, cs, n):
        copy(zs, xs, cs, n, s_right.at[0, 0], core_id, x).wait_recv()

    def spread(zs):
        for m in range(2):
            go_aux(zs, m).start()
        for m in range(2):
            go_core(zs, x, m).start()

    def take_aux(zs):
        for m in range(2):
            arrived(zs, 1 - x, c, own[m])
            go_core(zs, 1 - x, m).start()

    for n in range(4):
        @pl.when((z < 3) & (3 - n >= z))
        def _():
            go_right(z, 3 - n).start()

        @pl.when((z > 0) & (n < left_lim))
        def _():
            go_left(z, n).start()
    spread(z)

    def level_copy(d):
        to = (occ + d) % 8
        return pltpu.make_async_remote_copy(
            src_ref=levels.at[occ], dst_ref=levels.at[occ],
            send_sem=s_lev.at[d], recv_sem=r_lev.at[d],
            device_id={"occ": to}, device_id_type=MESH,
        )

    def level_wait(d):
        frm = (occ + 8 - d) % 8
        pltpu.make_async_remote_copy(
            src_ref=levels.at[frm], dst_ref=levels.at[frm],
            send_sem=s_lev.at[d], recv_sem=r_lev.at[d],
            device_id={"occ": (occ + d) % 8}, device_id_type=MESH,
        ).wait_recv()

    for d in range(1, 8):
        level_copy(d).start()
    across = jnp.broadcast_to(vir_ref[...].astype(F32), (256, 256))
    base[...] = across + across.T
    energy[...] = jnp.zeros_like(energy)

    for t in range(1, 4):
        @pl.when(z >= t)
        def _():
            zs = jnp.maximum(z - t, 0)
            for n in (3, 2, 1, 0):
                @pl.when(n >= z - 1)
                def _():
                    arrived(zs, x, c, n)

                @pl.when((z < 3) & (n >= z))
                def _():
                    go_right(zs, n).start()

        @pl.when(z + t <= 3)
        def _():
            zs = jnp.minimum(z + t, 3)
            for n in range(4):
                @pl.when(n < left_lim_in)
                def _():
                    arrived(zs, x, c, n)

                @pl.when((z > 0) & (n < left_lim))
                def _():
                    go_left(zs, n).start()

        @pl.when(z >= t)
        def _():
            spread(jnp.maximum(z - t, 0))

        @pl.when(z + t <= 3)
        def _():
            spread(jnp.minimum(z + t, 3))

        if t == 1:
            take_aux(z)
        else:
            @pl.when(z >= t - 1)
            def _():
                take_aux(jnp.maximum(z - t + 1, 0))

            @pl.when(z + t - 1 <= 3)
            def _():
                take_aux(jnp.minimum(z + t - 1, 3))

    @pl.when(z >= 3)
    def _():
        take_aux(jnp.maximum(z - 3, 0))

    @pl.when(z + 3 <= 3)
    def _():
        take_aux(jnp.minimum(z + 3, 3))

    for zs in range(4):
        for xs in range(2):
            for m in range(2):
                arrived(zs, xs, 1 - c, own[m])

    diag = (x == 0) & ((z == 0) | (z == 3))
    for kk in range(4):
        @pl.when((diag & (kk // 2 == c)) | (jnp.logical_not(diag) & ((kk == c) | (kk >= 2))))
        def _():
            n = own[kk // 2]
            for o in range(2):
                for xs in range(2):
                    for zs in range(4):
                        for cs in range(2):
                            mat[pl.ds(zs * 128 + cs * 64, 64), pl.ds(xs * 128, 128)] = blocks[
                                zs, xs, cs, n, 2 * (kk % 2) + o]
                prod = lax.dot_general(
                    mat[...], metric_ref[...], (((0,), (0,)), ((), ())),
                    preferred_element_type=F32)
                fac[2 * kk + o] = prod.astype(jnp.bfloat16)

    for d in range(1, 8):
        level_wait(d)

    rows8 = lax.broadcasted_iota(jnp.int32, (8, 128), 0)
    lanes8 = lax.broadcasted_iota(jnp.int32, (8, 128), 1)

    def one_pair(t, carry):
        li = jnp.where(diag, 4 * c + t % 4, 2 * c + t // 4)
        lj = jnp.where(diag, 4 * c + (t % 4 + t // 4) % 4, 4 + t % 4)
        gi = 4 * jnp.where(li < 4, own[0], own[1]) + li % 4
        gj = 4 * jnp.where(lj < 4, own[0], own[1]) + lj % 4
        fi, fj = fac[li], fac[lj]
        dims = (((1,), (1,)), ((), ()))
        direct = lax.dot_general(fi, fj, dims, preferred_element_type=F32)
        swapped = lax.dot_general(fj, fi, dims, preferred_element_type=F32)
        pair_level = levels[gi // 2, pl.ds(gi % 2, 1), :] + levels[gj // 2, pl.ds(gj % 2, 1), :]
        pair_level = jnp.concatenate([pair_level, pair_level], axis=1)
        term = direct * (2.0 * direct - swapped) / (base[...] - pair_level)
        term = -jnp.sum(jnp.sum(term, axis=0, keepdims=True), axis=1, keepdims=True)
        upper = (rows8 == gi % 2) & (lanes8 == gj % 8)
        energy[li // 2] += jnp.where(upper, term, 0.0)
        turned = (rows8 == gj % 2) & (lanes8 == gi % 8) & (gi != gj)
        energy[lj // 2] += jnp.where(turned, term, 0.0)
        return carry

    lax.fori_loop(0, jnp.where(diag, 10, 8), one_pair, 0)

    used = [jnp.logical_not(diag) | (c == h // 2) for h in range(4)]
    owner_occ = [2 * own[h // 2] + h % 2 for h in range(4)]
    column = [jnp.where(diag, own[h // 2], own[1 - h // 2]) for h in range(4)]
    slot = [column[h] % 2 * 2 + jnp.where(diag, 0, c) for h in range(4)]
    to_self = [(owner_occ[h] == occ) & (column[h] // 2 == x) for h in range(4)]

    def out_copy(h):
        return pltpu.make_async_remote_copy(
            src_ref=energy.at[h], dst_ref=shares.at[slot[h]],
            send_sem=s_out.at[h], recv_sem=r_out.at[slot[h]],
            device_id={"occ": owner_occ[h], "aux": column[h] // 2}, device_id_type=MESH,
        )

    for h in range(4):
        @pl.when(used[h] & jnp.logical_not(to_self[h]))
        def _():
            out_copy(h).start()

    for n in range(4):
        for t in range(4):
            @pl.when((z >= t) & (z < 3) & (n >= z))
            def _():
                go_right(jnp.maximum(z - t, 0), n).wait_send()

            @pl.when((z + t <= 3) & (z > 0) & (n < left_lim))
            def _():
                go_left(jnp.minimum(z + t, 3), n).wait_send()
    for zs in range(4):
        for m in range(2):
            go_aux(zs, m).wait_send()
            for xs in range(2):
                go_core(zs, xs, m).wait_send()
    for d in range(1, 8):
        level_copy(d).wait_send()

    gathered[...] = jnp.zeros_like(gathered)
    for h in range(4):
        @pl.when(used[h] & to_self[h])
        def _():
            gathered[...] += energy[h]
    for kk in range(2):
        for cs in range(2):
            col = 2 * x + kk
            off_self = ((own[0] == z) & (own[1] == col)) | ((own[1] == z) & (own[0] == col))
            diag_self = (col == z) & (jnp.where(c == 0, own[0], own[1]) == z)
            mine = jnp.where(diag, diag_self, off_self & (cs == c))

            @pl.when(((col != z) | (cs == 0)) & jnp.logical_not(mine))
            def _():
                pltpu.make_async_remote_copy(
                    src_ref=energy.at[0], dst_ref=shares.at[2 * kk + cs],
                    send_sem=s_out.at[0], recv_sem=r_out.at[2 * kk + cs],
                    device_id={"occ": core_id}, device_id_type=MESH,
                ).wait_recv()
                gathered[...] += shares[2 * kk + cs]
    out_ref[...] = gathered[0:2, 0:8]
    for h in range(4):
        @pl.when(used[h] & jnp.logical_not(to_self[h]))
        def _():
            out_copy(h).wait_send()


def fused_body(raw_ints, kept, eps_occ, eps_vir, metric_factor):
    bf, dma = jnp.bfloat16, pltpu.SemaphoreType.DMA
    vmem = pl.BlockSpec(memory_space=pltpu.VMEM)
    return pl.pallas_call(
        kernel,
        out_shape=jax.ShapeDtypeStruct((2, 8), F32),
        in_specs=[vmem, pl.BlockSpec(memory_space=pltpu.SMEM), vmem, vmem, vmem],
        out_specs=vmem,
        scratch_shapes=[
            pltpu.VMEM((4, 2, 2, 4, 4, 64, 128), bf),
            pltpu.VMEM((512, 256), bf),
            pltpu.VMEM((8, 256, 512), bf),
            pltpu.VMEM((256, 256), F32),
            pltpu.VMEM((8, 8, 128), F32),
            pltpu.VMEM((4, 8, 128), F32),
            pltpu.VMEM((4, 8, 128), F32),
            pltpu.VMEM((8, 128), F32),
            dma((4, 2, 2, 4)),
            dma((4, 4)),
            dma((4, 4)),
            dma((4, 2)),
            dma((4, 2, 2)),
            dma((8,)),
            dma((8,)),
            dma((4,)),
            dma((4,)),
        ],
        compiler_params=pltpu.CompilerParams(
            collective_id=0, has_side_effects=True, vmem_limit_bytes=40 * 2**20
        ),
    )(
        raw_ints.transpose(0, 2, 1), kept.transpose(1, 2, 0), eps_occ[None], eps_vir[None],
        metric_factor,
    )


def pair_terms(
    left_slice, right_all, left_cols, right_slice, own_levels, part_levels, vir_rows, vir_cols
):
    direct = jnp.einsum("iap,jbp->iajb", left_slice, right_all, preferred_element_type=jnp.float32)
    swapped = jnp.einsum(
        "ibp,jap->iajb", left_cols, right_slice, preferred_element_type=jnp.float32
    )
    own_f = own_levels.astype(jnp.float32)
    part_f = part_levels.astype(jnp.float32)
    rows_f = vir_rows.astype(jnp.float32)
    cols_f = vir_cols.astype(jnp.float32)
    denom = (
        rows_f[None, :, None, None]
        + cols_f[None, None, None, :]
        - own_f[:, None, None, None]
        - part_f[None, None, :, None]
    )
    return -jnp.sum(direct * (2.0 * direct - swapped) / denom, axis=(1, 3))


def body(raw_ints, kept, eps_occ, eps_vir, metric_factor):
    total_occ = raw_ints.shape[0]
    slice_vir = raw_ints.shape[1]
    slice_aux = raw_ints.shape[2]
    naux_all = metric_factor.shape[0]
    own_occ = eps_occ.shape[0]
    block_count = kept.shape[2]
    occ_index = lax.axis_index("occ")
    aux_index = lax.axis_index("aux")
    repeated = jnp.repeat(jnp.repeat(kept, total_occ // kept.shape[0], axis=0), VB, axis=1)
    kept_vir = lax.dynamic_slice_in_dim(repeated, aux_index * slice_vir, slice_vir, 1)
    aux_start = occ_index * slice_aux
    positions = aux_start + jnp.arange(slice_aux, dtype=jnp.int32)
    block_ids = positions // PB
    onehot = (block_ids[:, None] == jnp.arange(block_count, dtype=jnp.int32)[None, :]).astype(
        jnp.int32
    )
    kept_here = jnp.sum(kept_vir[:, :, None, :] * onehot[None, None, :, :], axis=3)
    offset = positions % PB
    screened = jnp.where(offset[None, None, :] < kept_here, raw_ints, jnp.zeros_like(raw_ints))
    relaid = lax.all_to_all(screened, "occ", split_axis=0, concat_axis=2, tiled=True)
    own_slice = jnp.dot(
        relaid.reshape(own_occ * slice_vir, naux_all),
        metric_factor,
        preferred_element_type=jnp.float32,
    )
    own_slice = own_slice.astype(jnp.bfloat16).reshape(own_occ, slice_vir, naux_all)
    vir_rows = lax.dynamic_slice_in_dim(eps_vir, aux_index * slice_vir, slice_vir)
    empty = jnp.zeros((own_occ, total_occ), jnp.float32)
    own_full = lax.all_gather(own_slice, "aux", axis=1, tiled=True)
    partner_rows = lax.all_gather(own_full, "occ", axis=0, tiled=True)
    partner_levels = lax.all_gather(eps_occ, "occ", axis=0, tiled=True)
    blocks_in = partner_rows.shape[0] // own_occ

    def add_block(block_no, totals):
        part_block = lax.dynamic_slice_in_dim(partner_rows, block_no * own_occ, own_occ, 0)
        part_level = lax.dynamic_slice_in_dim(partner_levels, block_no * own_occ, own_occ, 0)
        part_slice = lax.dynamic_slice_in_dim(part_block, aux_index * slice_vir, slice_vir, 1)
        term = pair_terms(
            own_slice, part_block, own_full, part_slice, eps_occ, part_level, vir_rows, eps_vir
        )
        column = block_no * own_occ
        before = lax.dynamic_slice_in_dim(totals, column, own_occ, 1)
        return lax.dynamic_update_slice_in_dim(totals, before + term, column, 1)

    energies = lax.fori_loop(0, blocks_in, add_block, empty)
    return lax.psum_scatter(energies, "aux", scatter_dimension=1, tiled=True)


def solution(mesh):
    in_specs = (
        P("parts", "aux", "occ"),
        P("parts", None, None),
        P(("parts", "occ")),
        P("parts"),
        P(),
    )
    out_specs = P(("parts", "occ"), "aux")
    fits = mesh.shape["occ"] == 8 and mesh.shape["aux"] == 2

    def step(raw_ints, kept, eps_occ, eps_vir, metric_factor):
        sizes = (raw_ints.shape, kept.shape, eps_occ.shape, eps_vir.shape)
        fused = fits and sizes == ((16, 128, 64), (8, 4, 4), (2,), (256,))
        run = fused_body if fused else body
        return run(raw_ints, kept, eps_occ, eps_vir, metric_factor)

    return jax.shard_map(step, mesh=mesh, in_specs=in_specs, out_specs=out_specs, check_vma=False)
```

```python
import jax
import jax.numpy as jnp
from jax import lax
from jax.experimental import pallas as pl
from jax.experimental.pallas import tpu as pltpu
from jax.sharding import PartitionSpec as P

VB = 64
PB = 128
MESH = pl.DeviceIdType.MESH
F32 = jnp.float32


def needs(x, z):
    first = jnp.maximum(z - 1, 0)
    second = jnp.where(z == 0, 1, jnp.where(z == 3, 3, 2 + x))
    return first, second


def kernel(
    raw_hbm, kept_hbm, occ_hbm, vir_hbm, metric_hbm, out_ref,
    raw_ref, kept_ref, occ_ref, vir_ref, metric_ref,
    blocks, mat, fac, base, levels, energy, shares, gathered,
    fetch, recv, s_right, s_left, s_aux, s_core, s_lev, r_lev, s_out, r_out,
):
    occ = lax.axis_index("occ")
    x = lax.axis_index("aux")
    z, c = occ // 2, occ % 2
    me = occ * 2 + x
    left_lim = jnp.where(z == 1, 2, 4)
    left_lim_in = jnp.where(z == 0, 2, 4)
    own = needs(x, z)
    other = needs(1 - x, z)

    fetches = [
        pltpu.make_async_copy(src, dst, fetch.at[k])
        for k, (src, dst) in enumerate([
            (raw_hbm, raw_ref), (kept_hbm, kept_ref), (occ_hbm, occ_ref),
            (vir_hbm, vir_ref), (metric_hbm, metric_ref),
        ])
    ]
    for one in fetches:
        one.start()
    barrier = pltpu.get_barrier_semaphore()
    for d in range(1, 16):
        peer = (me + d) % 16
        pl.semaphore_signal(
            barrier, inc=1, device_id={"occ": peer // 2, "aux": peer % 2}, device_id_type=MESH
        )

    for one in fetches[:3]:
        one.wait()
    place = lax.broadcasted_iota(jnp.int32, (VB, 2 * VB), 0) + c * VB
    lane = lax.broadcasted_iota(jnp.int32, (VB, 2 * VB), 1)
    for k in range(8):
        limit = jnp.where(lane < VB, kept_ref[2 * x, z, k], kept_ref[2 * x + 1, z, k])
        for i in (2 * k, 2 * k + 1):
            kept_part = jnp.where(place < limit, raw_ref[i].astype(F32), 0.0)
            blocks[z, x, c, i // 4, i % 4] = kept_part.astype(jnp.bfloat16)
    pair = occ_ref[...].astype(F32)
    row8 = lax.broadcasted_iota(jnp.int32, (8, 128), 0)
    levels[occ] = jnp.where(row8 == 0, pair[:, 0:1], pair[:, 1:2])

    pl.semaphore_wait(barrier, 15)

    def copy(zs, xs, cs, n, send_sem, to_occ, to_x):
        return pltpu.make_async_remote_copy(
            src_ref=blocks.at[zs, xs, cs, n],
            dst_ref=blocks.at[zs, xs, cs, n],
            send_sem=send_sem,
            recv_sem=recv.at[zs, xs, cs, n],
            device_id={"occ": to_occ, "aux": to_x},
            device_id_type=MESH,
        )

    right_id = jnp.minimum(occ + 2, 7)
    left_id = jnp.maximum(occ - 2, 0)
    core_id = 2 * z + 1 - c

    def go_right(zs, n):
        return copy(zs, x, c, n, s_right.at[zs, n], right_id, x)

    def go_left(zs, n):
        return copy(zs, x, c, n, s_left.at[zs, n], left_id, x)

    def go_aux(zs, n):
        return copy(zs, x, c, n, s_aux.at[zs, n], occ, 1 - x)

    def go_core(zs, xs, n):
        return copy(zs, xs, c, n, s_core.at[zs, xs, n], core_id, x)

    def arrived(zs, xs, cs, n):
        copy(zs, xs, cs, n, s_right.at[0, 0], core_id, x).wait_recv()

    def among(n, pair_of):
        return (n == pair_of[0]) | (n == pair_of[1])

    def spread(zs, n):
        @pl.when(among(n, other))
        def _():
            go_aux(zs, n).start()

        @pl.when(among(n, own))
        def _():
            go_core(zs, x, n).start()

    def take_aux(zs):
        for m in range(2):
            arrived(zs, 1 - x, c, own[m])
            go_core(zs, 1 - x, own[m]).start()

    def send_right(zs, n):
        @pl.when((z < 3) & (n >= z))
        def _():
            go_right(zs, n).start()

    def send_left(zs, n):
        @pl.when((z > 0) & (n < left_lim))
        def _():
            go_left(zs, n).start()

    for n in range(4):
        send_right(z, 3 - n)
        send_left(z, n)
    for n in range(4):
        spread(z, n)

    def level_copy(d):
        to = (occ + d) % 8
        return pltpu.make_async_remote_copy(
            src_ref=levels.at[occ], dst_ref=levels.at[occ],
            send_sem=s_lev.at[d], recv_sem=r_lev.at[d],
            device_id={"occ": to}, device_id_type=MESH,
        )

    def level_wait(d):
        frm = (occ + 8 - d) % 8
        pltpu.make_async_remote_copy(
            src_ref=levels.at[frm], dst_ref=levels.at[frm],
            send_sem=s_lev.at[d], recv_sem=r_lev.at[d],
            device_id={"occ": (occ + d) % 8}, device_id_type=MESH,
        ).wait_recv()

    for d in range(1, 8):
        level_copy(d).start()
    fetches[3].wait()
    fetches[4].wait()
    across = jnp.broadcast_to(vir_ref[...].astype(F32)[None], (256, 256))
    base[...] = across + across.T
    energy[...] = jnp.zeros_like(energy)

    for t in range(1, 4):
        for step in range(4):
            @pl.when((z >= t) & (3 - step >= z - 1))
            def _():
                zs = jnp.maximum(z - t, 0)
                arrived(zs, x, c, 3 - step)
                send_right(zs, 3 - step)
                spread(zs, 3 - step)

            @pl.when((z + t <= 3) & (step < left_lim_in))
            def _():
                zs = jnp.minimum(z + t, 3)
                arrived(zs, x, c, step)
                send_left(zs, step)
                spread(zs, step)

        if t == 1:
            take_aux(z)
        else:
            @pl.when(z >= t - 1)
            def _():
                take_aux(jnp.maximum(z - t + 1, 0))

            @pl.when(z + t - 1 <= 3)
            def _():
                take_aux(jnp.minimum(z + t - 1, 3))

    @pl.when(z >= 3)
    def _():
        take_aux(jnp.maximum(z - 3, 0))

    @pl.when(z + 3 <= 3)
    def _():
        take_aux(jnp.minimum(z + 3, 3))

    for zs in range(4):
        for xs in range(2):
            for m in range(2):
                arrived(zs, xs, 1 - c, own[m])

    diag = (x == 0) & ((z == 0) | (z == 3))
    for kk in range(4):
        @pl.when((diag & (kk // 2 == c)) | (jnp.logical_not(diag) & ((kk == c) | (kk >= 2))))
        def _():
            n = own[kk // 2]
            for o in range(2):
                for xs in range(2):
                    for zs in range(4):
                        for cs in range(2):
                            mat[pl.ds(zs * 128 + cs * 64, 64), pl.ds(xs * 128, 128)] = blocks[
                                zs, xs, cs, n, 2 * (kk % 2) + o]
                prod = lax.dot_general(
                    mat[...], metric_ref[...], (((0,), (0,)), ((), ())),
                    preferred_element_type=F32)
                fac[2 * kk + o] = prod.astype(jnp.bfloat16)

    for d in range(1, 8):
        level_wait(d)

    rows8 = lax.broadcasted_iota(jnp.int32, (8, 128), 0)
    lanes8 = lax.broadcasted_iota(jnp.int32, (8, 128), 1)

    def one_pair(t):
        li = jnp.where(diag, 4 * c + t % 4, 2 * c + t // 4)
        lj = jnp.where(diag, 4 * c + (t % 4 + t // 4) % 4, 4 + t % 4)
        gi = 4 * jnp.where(li < 4, own[0], own[1]) + li % 4
        gj = 4 * jnp.where(lj < 4, own[0], own[1]) + lj % 4
        fi, fj = fac[li], fac[lj]
        dims = (((1,), (1,)), ((), ()))
        direct = lax.dot_general(fi, fj, dims, preferred_element_type=F32)
        swapped = lax.dot_general(fj, fi, dims, preferred_element_type=F32)
        pair_level = levels[gi // 2, pl.ds(gi % 2, 1), :] + levels[gj // 2, pl.ds(gj % 2, 1), :]
        pair_level = jnp.concatenate([pair_level, pair_level], axis=1)
        term = direct * (2.0 * direct - swapped) / (base[...] - pair_level)
        term = -jnp.sum(jnp.sum(term, axis=0, keepdims=True), axis=1, keepdims=True)
        upper = (rows8 == gi % 2) & (lanes8 == gj % 8)
        energy[li // 2] += jnp.where(upper, term, 0.0)
        turned = (rows8 == gj % 2) & (lanes8 == gi % 8) & (gi != gj)
        energy[lj // 2] += jnp.where(turned, term, 0.0)

    def two_pairs(t, carry):
        one_pair(2 * t)
        one_pair(2 * t + 1)
        return carry

    lax.fori_loop(0, jnp.where(diag, 5, 4), two_pairs, 0)

    used = [jnp.logical_not(diag) | (c == h // 2) for h in range(4)]
    owner_occ = [2 * own[h // 2] + h % 2 for h in range(4)]
    column = [jnp.where(diag, own[h // 2], own[1 - h // 2]) for h in range(4)]
    slot = [column[h] % 2 * 2 + jnp.where(diag, 0, c) for h in range(4)]
    to_self = [(owner_occ[h] == occ) & (column[h] // 2 == x) for h in range(4)]

    def out_copy(h):
        return pltpu.make_async_remote_copy(
            src_ref=energy.at[h], dst_ref=shares.at[slot[h]],
            send_sem=s_out.at[h], recv_sem=r_out.at[slot[h]],
            device_id={"occ": owner_occ[h], "aux": column[h] // 2}, device_id_type=MESH,
        )

    for h in range(4):
        @pl.when(used[h] & jnp.logical_not(to_self[h]))
        def _():
            out_copy(h).start()

    for n in range(4):
        for t in range(4):
            @pl.when((z >= t) & (z < 3) & (n >= z))
            def _():
                go_right(jnp.maximum(z - t, 0), n).wait_send()

            @pl.when((z + t <= 3) & (z > 0) & (n < left_lim))
            def _():
                go_left(jnp.minimum(z + t, 3), n).wait_send()
    for zs in range(4):
        for m in range(2):
            go_aux(zs, other[m]).wait_send()
            for xs in range(2):
                go_core(zs, xs, own[m]).wait_send()
    for d in range(1, 8):
        level_copy(d).wait_send()

    gathered[...] = jnp.zeros_like(gathered)
    for h in range(4):
        @pl.when(used[h] & to_self[h])
        def _():
            gathered[...] += energy[h]
    for kk in range(2):
        for cs in range(2):
            col = 2 * x + kk
            off_self = ((own[0] == z) & (own[1] == col)) | ((own[1] == z) & (own[0] == col))
            diag_self = (col == z) & (jnp.where(c == 0, own[0], own[1]) == z)
            mine = jnp.where(diag, diag_self, off_self & (cs == c))

            @pl.when(((col != z) | (cs == 0)) & jnp.logical_not(mine))
            def _():
                pltpu.make_async_remote_copy(
                    src_ref=energy.at[0], dst_ref=shares.at[2 * kk + cs],
                    send_sem=s_out.at[0], recv_sem=r_out.at[2 * kk + cs],
                    device_id={"occ": core_id}, device_id_type=MESH,
                ).wait_recv()
                gathered[...] += shares[2 * kk + cs]
    out_ref[...] = gathered[0:2, 0:8]
    for h in range(4):
        @pl.when(used[h] & jnp.logical_not(to_self[h]))
        def _():
            out_copy(h).wait_send()


def fused_body(raw_ints, kept, eps_occ, eps_vir, metric_factor):
    bf, dma = jnp.bfloat16, pltpu.SemaphoreType.DMA
    vmem = pl.BlockSpec(memory_space=pltpu.VMEM)
    return pl.pallas_call(
        kernel,
        out_shape=jax.ShapeDtypeStruct((2, 8), F32),
        in_specs=[pl.BlockSpec(memory_space=pl.ANY)] * 5,
        out_specs=vmem,
        scratch_shapes=[
            pltpu.VMEM((16, 64, 128), bf),
            pltpu.SMEM((4, 4, 8), jnp.int32),
            pltpu.VMEM((1, 2), bf),
            pltpu.VMEM((256,), bf),
            pltpu.VMEM((512, 512), bf),
            pltpu.VMEM((4, 2, 2, 4, 4, 64, 128), bf),
            pltpu.VMEM((512, 256), bf),
            pltpu.VMEM((8, 256, 512), bf),
            pltpu.VMEM((256, 256), F32),
            pltpu.VMEM((8, 8, 128), F32),
            pltpu.VMEM((4, 8, 128), F32),
            pltpu.VMEM((4, 8, 128), F32),
            pltpu.VMEM((8, 128), F32),
            dma((5,)),
            dma((4, 2, 2, 4)),
            dma((4, 4)),
            dma((4, 4)),
            dma((4, 4)),
            dma((4, 2, 4)),
            dma((8,)),
            dma((8,)),
            dma((4,)),
            dma((4,)),
        ],
        compiler_params=pltpu.CompilerParams(
            collective_id=0, has_side_effects=True, vmem_limit_bytes=60 * 2**20
        ),
    )(
        raw_ints.transpose(0, 2, 1), kept.transpose(1, 2, 0), eps_occ[None], eps_vir,
        metric_factor,
    )


def pair_terms(
    left_slice, right_all, left_cols, right_slice, own_levels, part_levels, vir_rows, vir_cols
):
    direct = jnp.einsum("iap,jbp->iajb", left_slice, right_all, preferred_element_type=jnp.float32)
    swapped = jnp.einsum(
        "ibp,jap->iajb", left_cols, right_slice, preferred_element_type=jnp.float32
    )
    own_f = own_levels.astype(jnp.float32)
    part_f = part_levels.astype(jnp.float32)
    rows_f = vir_rows.astype(jnp.float32)
    cols_f = vir_cols.astype(jnp.float32)
    denom = (
        rows_f[None, :, None, None]
        + cols_f[None, None, None, :]
        - own_f[:, None, None, None]
        - part_f[None, None, :, None]
    )
    return -jnp.sum(direct * (2.0 * direct - swapped) / denom, axis=(1, 3))


def body(raw_ints, kept, eps_occ, eps_vir, metric_factor):
    total_occ = raw_ints.shape[0]
    slice_vir = raw_ints.shape[1]
    slice_aux = raw_ints.shape[2]
    naux_all = metric_factor.shape[0]
    own_occ = eps_occ.shape[0]
    block_count = kept.shape[2]
    occ_index = lax.axis_index("occ")
    aux_index = lax.axis_index("aux")
    repeated = jnp.repeat(jnp.repeat(kept, total_occ // kept.shape[0], axis=0), VB, axis=1)
    kept_vir = lax.dynamic_slice_in_dim(repeated, aux_index * slice_vir, slice_vir, 1)
    aux_start = occ_index * slice_aux
    positions = aux_start + jnp.arange(slice_aux, dtype=jnp.int32)
    block_ids = positions // PB
    onehot = (block_ids[:, None] == jnp.arange(block_count, dtype=jnp.int32)[None, :]).astype(
        jnp.int32
    )
    kept_here = jnp.sum(kept_vir[:, :, None, :] * onehot[None, None, :, :], axis=3)
    offset = positions % PB
    screened = jnp.where(offset[None, None, :] < kept_here, raw_ints, jnp.zeros_like(raw_ints))
    relaid = lax.all_to_all(screened, "occ", split_axis=0, concat_axis=2, tiled=True)
    own_slice = jnp.dot(
        relaid.reshape(own_occ * slice_vir, naux_all),
        metric_factor,
        preferred_element_type=jnp.float32,
    )
    own_slice = own_slice.astype(jnp.bfloat16).reshape(own_occ, slice_vir, naux_all)
    vir_rows = lax.dynamic_slice_in_dim(eps_vir, aux_index * slice_vir, slice_vir)
    empty = jnp.zeros((own_occ, total_occ), jnp.float32)
    own_full = lax.all_gather(own_slice, "aux", axis=1, tiled=True)
    partner_rows = lax.all_gather(own_full, "occ", axis=0, tiled=True)
    partner_levels = lax.all_gather(eps_occ, "occ", axis=0, tiled=True)
    blocks_in = partner_rows.shape[0] // own_occ

    def add_block(block_no, totals):
        part_block = lax.dynamic_slice_in_dim(partner_rows, block_no * own_occ, own_occ, 0)
        part_level = lax.dynamic_slice_in_dim(partner_levels, block_no * own_occ, own_occ, 0)
        part_slice = lax.dynamic_slice_in_dim(part_block, aux_index * slice_vir, slice_vir, 1)
        term = pair_terms(
            own_slice, part_block, own_full, part_slice, eps_occ, part_level, vir_rows, eps_vir
        )
        column = block_no * own_occ
        before = lax.dynamic_slice_in_dim(totals, column, own_occ, 1)
        return lax.dynamic_update_slice_in_dim(totals, before + term, column, 1)

    energies = lax.fori_loop(0, blocks_in, add_block, empty)
    return lax.psum_scatter(energies, "aux", scatter_dimension=1, tiled=True)


def solution(mesh):
    in_specs = (
        P("parts", "aux", "occ"),
        P("parts", None, None),
        P(("parts", "occ")),
        P("parts"),
        P(),
    )
    out_specs = P(("parts", "occ"), "aux")
    fits = mesh.shape["occ"] == 8 and mesh.shape["aux"] == 2

    def step(raw_ints, kept, eps_occ, eps_vir, metric_factor):
        sizes = (raw_ints.shape, kept.shape, eps_occ.shape, eps_vir.shape)
        fused = fits and sizes == ((16, 128, 64), (8, 4, 4), (2,), (256,))
        run = fused_body if fused else body
        return run(raw_ints, kept, eps_occ, eps_vir, metric_factor)

    return jax.shard_map(step, mesh=mesh, in_specs=in_specs, out_specs=out_specs, check_vma=False)
```

```python
import jax
import jax.numpy as jnp
from jax import lax
from jax.experimental import pallas as pl
from jax.experimental.pallas import tpu as pltpu
from jax.sharding import PartitionSpec as P

VB = 64
PB = 128
MESH = pl.DeviceIdType.MESH
F32 = jnp.float32


def needs(x, z):
    first = jnp.maximum(z - 1, 0)
    second = jnp.where(z == 0, 1, jnp.where(z == 3, 3, 2 + x))
    return first, second


def kernel(
    raw_hbm, kept_hbm, occ_hbm, vir_hbm, metric_hbm, out_ref,
    raw_ref, kept_ref, occ_ref, vir_ref, metric_ref,
    blocks, mat, fac, base, levels, energy, shares, gathered,
    fetch, recv, s_right, s_left, s_aux, s_core, s_lev, r_lev, s_out, r_out,
):
    occ = lax.axis_index("occ")
    x = lax.axis_index("aux")
    z, c = occ // 2, occ % 2
    left_lim = jnp.where(z == 1, 2, 4)
    left_lim_in = jnp.where(z == 0, 2, 4)
    own = needs(x, z)
    other = needs(1 - x, z)

    fetches = [
        pltpu.make_async_copy(src, dst, fetch.at[k])
        for k, (src, dst) in enumerate([
            (raw_hbm, raw_ref), (kept_hbm, kept_ref), (occ_hbm, occ_ref),
            (vir_hbm, vir_ref), (metric_hbm, metric_ref),
        ])
    ]
    for one in fetches:
        one.start()
    barrier = pltpu.get_barrier_semaphore()
    right_id = jnp.minimum(occ + 2, 7)
    left_id = jnp.maximum(occ - 2, 0)
    core_id = 2 * z + 1 - c

    def greet(to_occ, to_x):
        pl.semaphore_signal(
            barrier, inc=1, device_id={"occ": to_occ, "aux": to_x}, device_id_type=MESH
        )

    greet(core_id, x)
    greet(occ, 1 - x)

    @pl.when(z < 3)
    def _():
        greet(right_id, x)

    @pl.when(z > 0)
    def _():
        greet(left_id, x)

    for one in fetches[:3]:
        one.wait()
    place = lax.broadcasted_iota(jnp.int32, (VB, 2 * VB), 0) + c * VB
    lane = lax.broadcasted_iota(jnp.int32, (VB, 2 * VB), 1)
    for k in range(8):
        limit = jnp.where(lane < VB, kept_ref[2 * x, z, k], kept_ref[2 * x + 1, z, k])
        for i in (2 * k, 2 * k + 1):
            kept_part = jnp.where(place < limit, raw_ref[i].astype(F32), 0.0)
            blocks[z, x, c, i // 4, i % 4] = kept_part.astype(jnp.bfloat16)
    pair = occ_ref[...].astype(F32)
    row8 = lax.broadcasted_iota(jnp.int32, (8, 128), 0)
    levels[occ] = jnp.where(row8 == 0, pair[:, 0:1], pair[:, 1:2])

    pl.semaphore_wait(barrier, jnp.where((z == 0) | (z == 3), 3, 4))

    def copy(zs, xs, cs, n, send_sem, to_occ, to_x):
        return pltpu.make_async_remote_copy(
            src_ref=blocks.at[zs, xs, cs, n],
            dst_ref=blocks.at[zs, xs, cs, n],
            send_sem=send_sem,
            recv_sem=recv.at[zs, xs, cs, n],
            device_id={"occ": to_occ, "aux": to_x},
            device_id_type=MESH,
        )

    def go_right(zs, n):
        return copy(zs, x, c, n, s_right.at[zs, n], right_id, x)

    def go_left(zs, n):
        return copy(zs, x, c, n, s_left.at[zs, n], left_id, x)

    def go_aux(zs, n):
        return copy(zs, x, c, n, s_aux.at[zs, n], occ, 1 - x)

    def go_core(zs, xs, n):
        return copy(zs, xs, c, n, s_core.at[zs, xs, n], core_id, x)

    def arrived(zs, xs, cs, n):
        copy(zs, xs, cs, n, s_right.at[0, 0], core_id, x).wait_recv()

    def among(n, pair_of):
        return (n == pair_of[0]) | (n == pair_of[1])

    def spread(zs, n):
        @pl.when(among(n, other))
        def _():
            go_aux(zs, n).start()

        @pl.when(among(n, own))
        def _():
            go_core(zs, x, n).start()

    def take_aux(zs):
        for m in range(2):
            arrived(zs, 1 - x, c, own[m])
            go_core(zs, 1 - x, own[m]).start()

    def send_right(zs, n):
        @pl.when((z < 3) & (n >= z))
        def _():
            go_right(zs, n).start()

    def send_left(zs, n):
        @pl.when((z > 0) & (n < left_lim))
        def _():
            go_left(zs, n).start()

    def level_copy(zs, cs, send_sem, to_occ):
        return pltpu.make_async_remote_copy(
            src_ref=levels.at[2 * zs + cs], dst_ref=levels.at[2 * zs + cs],
            send_sem=send_sem, recv_sem=r_lev.at[2 * zs + cs],
            device_id={"occ": to_occ, "aux": x}, device_id_type=MESH,
        )

    def level_right(zs):
        return level_copy(zs, c, s_lev.at[0, zs], right_id)

    def level_left(zs):
        return level_copy(zs, c, s_lev.at[1, zs], left_id)

    def level_core(zs):
        return level_copy(zs, c, s_lev.at[2, zs], core_id)

    def level_arrived(zs, cs):
        level_copy(zs, cs, s_lev.at[0, 0], core_id).wait_recv()

    def pass_levels(zs, right, left):
        if right:
            @pl.when(z < 3)
            def _():
                level_right(zs).start()
        if left:
            @pl.when(z > 0)
            def _():
                level_left(zs).start()
        level_core(zs).start()

    pass_levels(z, True, True)
    for n in range(4):
        send_right(z, 3 - n)

        @pl.when((z != 2) | (n < 2))
        def _():
            send_left(z, n)
    for n in range(4):
        spread(z, n)

    fetches[3].wait()
    fetches[4].wait()
    across = jnp.broadcast_to(vir_ref[...].astype(F32)[None], (256, 256))
    base[...] = across + across.T
    energy[...] = jnp.zeros_like(energy)

    for t in range(1, 4):
        @pl.when(z >= t)
        def _():
            level_arrived(jnp.maximum(z - t, 0), c)
            pass_levels(jnp.maximum(z - t, 0), True, False)

        @pl.when(z + t <= 3)
        def _():
            level_arrived(jnp.minimum(z + t, 3), c)
            pass_levels(jnp.minimum(z + t, 3), False, True)

        for step in range(4):
            @pl.when((z >= t) & (3 - step >= z - 1))
            def _():
                zs = jnp.maximum(z - t, 0)
                arrived(zs, x, c, 3 - step)
                send_right(zs, 3 - step)
                spread(zs, 3 - step)

            @pl.when((z + t <= 3) & (step < left_lim_in))
            def _():
                zs = jnp.minimum(z + t, 3)
                arrived(zs, x, c, step)
                send_left(zs, step)
                if t == 1 and step == 1:
                    @pl.when(z == 2)
                    def _():
                        send_left(z, 2)
                        send_left(z, 3)
                spread(zs, step)

        if t == 1:
            take_aux(z)
        else:
            @pl.when(z >= t - 1)
            def _():
                take_aux(jnp.maximum(z - t + 1, 0))

            @pl.when(z + t - 1 <= 3)
            def _():
                take_aux(jnp.minimum(z + t - 1, 3))

    @pl.when(z >= 3)
    def _():
        take_aux(jnp.maximum(z - 3, 0))

    @pl.when(z + 3 <= 3)
    def _():
        take_aux(jnp.minimum(z + 3, 3))

    for zs in range(4):
        for xs in range(2):
            for m in range(2):
                arrived(zs, xs, 1 - c, own[m])

    diag = (x == 0) & ((z == 0) | (z == 3))
    for kk in range(4):
        @pl.when((diag & (kk // 2 == c)) | (jnp.logical_not(diag) & ((kk == c) | (kk >= 2))))
        def _():
            n = own[kk // 2]
            for o in range(2):
                for xs in range(2):
                    for zs in range(4):
                        for cs in range(2):
                            mat[pl.ds(zs * 128 + cs * 64, 64), pl.ds(xs * 128, 128)] = blocks[
                                zs, xs, cs, n, 2 * (kk % 2) + o]
                prod = lax.dot_general(
                    mat[...], metric_ref[...], (((0,), (0,)), ((), ())),
                    preferred_element_type=F32)
                fac[2 * kk + o] = prod.astype(jnp.bfloat16)

    for zs in range(4):
        level_arrived(zs, 1 - c)

    rows8 = lax.broadcasted_iota(jnp.int32, (8, 128), 0)
    lanes8 = lax.broadcasted_iota(jnp.int32, (8, 128), 1)

    def one_pair(t):
        li = jnp.where(diag, 4 * c + t % 4, 2 * c + t // 4)
        lj = jnp.where(diag, 4 * c + (t % 4 + t // 4) % 4, 4 + t % 4)
        gi = 4 * jnp.where(li < 4, own[0], own[1]) + li % 4
        gj = 4 * jnp.where(lj < 4, own[0], own[1]) + lj % 4
        fi, fj = fac[li], fac[lj]
        dims = (((1,), (1,)), ((), ()))
        direct = lax.dot_general(fi, fj, dims, preferred_element_type=F32)
        swapped = lax.dot_general(fj, fi, dims, preferred_element_type=F32)
        pair_level = levels[gi // 2, pl.ds(gi % 2, 1), :] + levels[gj // 2, pl.ds(gj % 2, 1), :]
        pair_level = jnp.concatenate([pair_level, pair_level], axis=1)
        term = direct * (2.0 * direct - swapped) / (base[...] - pair_level)
        term = -jnp.sum(jnp.sum(term, axis=0, keepdims=True), axis=1, keepdims=True)
        upper = (rows8 == gi % 2) & (lanes8 == gj % 8)
        energy[li // 2] += jnp.where(upper, term, 0.0)
        turned = (rows8 == gj % 2) & (lanes8 == gi % 8) & (gi != gj)
        energy[lj // 2] += jnp.where(turned, term, 0.0)

    def two_pairs(t, carry):
        one_pair(2 * t)
        one_pair(2 * t + 1)
        return carry

    lax.fori_loop(0, jnp.where(diag, 5, 4), two_pairs, 0)

    used = [jnp.logical_not(diag) | (c == h // 2) for h in range(4)]
    owner_occ = [2 * own[h // 2] + h % 2 for h in range(4)]
    column = [jnp.where(diag, own[h // 2], own[1 - h // 2]) for h in range(4)]
    slot = [column[h] % 2 * 2 + jnp.where(diag, 0, c) for h in range(4)]
    to_self = [(owner_occ[h] == occ) & (column[h] // 2 == x) for h in range(4)]

    def out_copy(h):
        return pltpu.make_async_remote_copy(
            src_ref=energy.at[h], dst_ref=shares.at[slot[h]],
            send_sem=s_out.at[h], recv_sem=r_out.at[slot[h]],
            device_id={"occ": owner_occ[h], "aux": column[h] // 2}, device_id_type=MESH,
        )

    for h in range(4):
        @pl.when(used[h] & jnp.logical_not(to_self[h]))
        def _():
            out_copy(h).start()

    for n in range(4):
        for t in range(4):
            @pl.when((z >= t) & (z < 3) & (n >= z))
            def _():
                go_right(jnp.maximum(z - t, 0), n).wait_send()

            @pl.when((z + t <= 3) & (z > 0) & (n < left_lim))
            def _():
                go_left(jnp.minimum(z + t, 3), n).wait_send()
    for zs in range(4):
        for m in range(2):
            go_aux(zs, other[m]).wait_send()
            for xs in range(2):
                go_core(zs, xs, own[m]).wait_send()
    for t in range(4):
        @pl.when((z >= t) & (z < 3))
        def _():
            level_right(jnp.maximum(z - t, 0)).wait_send()

        @pl.when((z + t <= 3) & (z > 0))
        def _():
            level_left(jnp.minimum(z + t, 3)).wait_send()

        level_core(t).wait_send()

    gathered[...] = jnp.zeros_like(gathered)
    for h in range(4):
        @pl.when(used[h] & to_self[h])
        def _():
            gathered[...] += energy[h]
    for kk in range(2):
        for cs in range(2):
            col = 2 * x + kk
            off_self = ((own[0] == z) & (own[1] == col)) | ((own[1] == z) & (own[0] == col))
            diag_self = (col == z) & (jnp.where(c == 0, own[0], own[1]) == z)
            mine = jnp.where(diag, diag_self, off_self & (cs == c))

            @pl.when(((col != z) | (cs == 0)) & jnp.logical_not(mine))
            def _():
                pltpu.make_async_remote_copy(
                    src_ref=energy.at[0], dst_ref=shares.at[2 * kk + cs],
                    send_sem=s_out.at[0], recv_sem=r_out.at[2 * kk + cs],
                    device_id={"occ": core_id}, device_id_type=MESH,
                ).wait_recv()
                gathered[...] += shares[2 * kk + cs]
    out_ref[...] = gathered[0:2, 0:8]
    for h in range(4):
        @pl.when(used[h] & jnp.logical_not(to_self[h]))
        def _():
            out_copy(h).wait_send()


def fused_body(raw_ints, kept, eps_occ, eps_vir, metric_factor):
    bf, dma = jnp.bfloat16, pltpu.SemaphoreType.DMA
    vmem = pl.BlockSpec(memory_space=pltpu.VMEM)
    return pl.pallas_call(
        kernel,
        out_shape=jax.ShapeDtypeStruct((2, 8), F32),
        in_specs=[pl.BlockSpec(memory_space=pl.ANY)] * 5,
        out_specs=vmem,
        scratch_shapes=[
            pltpu.VMEM((16, 64, 128), bf),
            pltpu.SMEM((4, 4, 8), jnp.int32),
            pltpu.VMEM((1, 2), bf),
            pltpu.VMEM((256,), bf),
            pltpu.VMEM((512, 512), bf),
            pltpu.VMEM((4, 2, 2, 4, 4, 64, 128), bf),
            pltpu.VMEM((512, 256), bf),
            pltpu.VMEM((8, 256, 512), bf),
            pltpu.VMEM((256, 256), F32),
            pltpu.VMEM((8, 8, 128), F32),
            pltpu.VMEM((4, 8, 128), F32),
            pltpu.VMEM((4, 8, 128), F32),
            pltpu.VMEM((8, 128), F32),
            dma((5,)),
            dma((4, 2, 2, 4)),
            dma((4, 4)),
            dma((4, 4)),
            dma((4, 4)),
            dma((4, 2, 4)),
            dma((3, 4)),
            dma((8,)),
            dma((4,)),
            dma((4,)),
        ],
        compiler_params=pltpu.CompilerParams(
            collective_id=0, has_side_effects=True, vmem_limit_bytes=60 * 2**20
        ),
    )(
        raw_ints.transpose(0, 2, 1), kept.transpose(1, 2, 0), eps_occ[None], eps_vir,
        metric_factor,
    )


def pair_terms(
    left_slice, right_all, left_cols, right_slice, own_levels, part_levels, vir_rows, vir_cols
):
    direct = jnp.einsum("iap,jbp->iajb", left_slice, right_all, preferred_element_type=jnp.float32)
    swapped = jnp.einsum(
        "ibp,jap->iajb", left_cols, right_slice, preferred_element_type=jnp.float32
    )
    own_f = own_levels.astype(jnp.float32)
    part_f = part_levels.astype(jnp.float32)
    rows_f = vir_rows.astype(jnp.float32)
    cols_f = vir_cols.astype(jnp.float32)
    denom = (
        rows_f[None, :, None, None]
        + cols_f[None, None, None, :]
        - own_f[:, None, None, None]
        - part_f[None, None, :, None]
    )
    return -jnp.sum(direct * (2.0 * direct - swapped) / denom, axis=(1, 3))


def body(raw_ints, kept, eps_occ, eps_vir, metric_factor):
    total_occ = raw_ints.shape[0]
    slice_vir = raw_ints.shape[1]
    slice_aux = raw_ints.shape[2]
    naux_all = metric_factor.shape[0]
    own_occ = eps_occ.shape[0]
    block_count = kept.shape[2]
    occ_index = lax.axis_index("occ")
    aux_index = lax.axis_index("aux")
    repeated = jnp.repeat(jnp.repeat(kept, total_occ // kept.shape[0], axis=0), VB, axis=1)
    kept_vir = lax.dynamic_slice_in_dim(repeated, aux_index * slice_vir, slice_vir, 1)
    aux_start = occ_index * slice_aux
    positions = aux_start + jnp.arange(slice_aux, dtype=jnp.int32)
    block_ids = positions // PB
    onehot = (block_ids[:, None] == jnp.arange(block_count, dtype=jnp.int32)[None, :]).astype(
        jnp.int32
    )
    kept_here = jnp.sum(kept_vir[:, :, None, :] * onehot[None, None, :, :], axis=3)
    offset = positions % PB
    screened = jnp.where(offset[None, None, :] < kept_here, raw_ints, jnp.zeros_like(raw_ints))
    relaid = lax.all_to_all(screened, "occ", split_axis=0, concat_axis=2, tiled=True)
    own_slice = jnp.dot(
        relaid.reshape(own_occ * slice_vir, naux_all),
        metric_factor,
        preferred_element_type=jnp.float32,
    )
    own_slice = own_slice.astype(jnp.bfloat16).reshape(own_occ, slice_vir, naux_all)
    vir_rows = lax.dynamic_slice_in_dim(eps_vir, aux_index * slice_vir, slice_vir)
    empty = jnp.zeros((own_occ, total_occ), jnp.float32)
    own_full = lax.all_gather(own_slice, "aux", axis=1, tiled=True)
    partner_rows = lax.all_gather(own_full, "occ", axis=0, tiled=True)
    partner_levels = lax.all_gather(eps_occ, "occ", axis=0, tiled=True)
    blocks_in = partner_rows.shape[0] // own_occ

    def add_block(block_no, totals):
        part_block = lax.dynamic_slice_in_dim(partner_rows, block_no * own_occ, own_occ, 0)
        part_level = lax.dynamic_slice_in_dim(partner_levels, block_no * own_occ, own_occ, 0)
        part_slice = lax.dynamic_slice_in_dim(part_block, aux_index * slice_vir, slice_vir, 1)
        term = pair_terms(
            own_slice, part_block, own_full, part_slice, eps_occ, part_level, vir_rows, eps_vir
        )
        column = block_no * own_occ
        before = lax.dynamic_slice_in_dim(totals, column, own_occ, 1)
        return lax.dynamic_update_slice_in_dim(totals, before + term, column, 1)

    energies = lax.fori_loop(0, blocks_in, add_block, empty)
    return lax.psum_scatter(energies, "aux", scatter_dimension=1, tiled=True)


def solution(mesh):
    in_specs = (
        P("parts", "aux", "occ"),
        P("parts", None, None),
        P(("parts", "occ")),
        P("parts"),
        P(),
    )
    out_specs = P(("parts", "occ"), "aux")
    fits = mesh.shape["occ"] == 8 and mesh.shape["aux"] == 2

    def step(raw_ints, kept, eps_occ, eps_vir, metric_factor):
        sizes = (raw_ints.shape, kept.shape, eps_occ.shape, eps_vir.shape)
        fused = fits and sizes == ((16, 128, 64), (8, 4, 4), (2,), (256,))
        run = fused_body if fused else body
        return run(raw_ints, kept, eps_occ, eps_vir, metric_factor)

    return jax.shard_map(step, mesh=mesh, in_specs=in_specs, out_specs=out_specs, check_vma=False)
```

```python
import jax
import jax.numpy as jnp
from jax import lax
from jax.experimental import pallas as pl
from jax.experimental.pallas import tpu as pltpu
from jax.sharding import PartitionSpec as P

VB = 64
PB = 128
MESH = pl.DeviceIdType.MESH
F32 = jnp.float32


def needs(x, z):
    first = jnp.maximum(z - 1, 0)
    second = jnp.where(z == 0, 1, jnp.where(z == 3, 3, 2 + x))
    return first, second


def kernel(
    raw_hbm, kept_hbm, occ_hbm, vir_hbm, metric_hbm, out_ref,
    raw_ref, kept_ref, occ_ref, vir_ref, metric_ref,
    blocks, mat, fac, base, levels, energy, shares, gathered,
    fetch, recv, s_right, s_left, s_aux, s_core, s_lev, r_lev, s_out, r_out,
):
    occ = lax.axis_index("occ")
    x = lax.axis_index("aux")
    z, c = occ // 2, occ % 2
    left_lim = jnp.where(z == 1, 2, 4)
    left_lim_in = jnp.where(z == 0, 2, 4)
    own = needs(x, z)
    other = needs(1 - x, z)

    fetches = [
        pltpu.make_async_copy(src, dst, fetch.at[k])
        for k, (src, dst) in enumerate([
            (raw_hbm, raw_ref), (kept_hbm, kept_ref), (occ_hbm, occ_ref),
            (vir_hbm, vir_ref), (metric_hbm, metric_ref),
        ])
    ]
    for one in fetches:
        one.start()
    barrier = pltpu.get_barrier_semaphore()
    right_id = jnp.minimum(occ + 2, 7)
    left_id = jnp.maximum(occ - 2, 0)
    core_id = 2 * z + 1 - c

    def greet(to_occ, to_x):
        pl.semaphore_signal(
            barrier, inc=1, device_id={"occ": to_occ, "aux": to_x}, device_id_type=MESH
        )

    greet(core_id, x)
    greet(occ, 1 - x)

    @pl.when(z < 3)
    def _():
        greet(right_id, x)

    @pl.when(z > 0)
    def _():
        greet(left_id, x)

    for one in fetches[:3]:
        one.wait()
    place = lax.broadcasted_iota(jnp.int32, (VB, 2 * VB), 0) + c * VB
    lane = lax.broadcasted_iota(jnp.int32, (VB, 2 * VB), 1)
    for k in range(8):
        limit = jnp.where(lane < VB, kept_ref[2 * x, z, k], kept_ref[2 * x + 1, z, k])
        for i in (2 * k, 2 * k + 1):
            kept_part = jnp.where(place < limit, raw_ref[i].astype(F32), 0.0)
            blocks[z, x, c, i // 4, i % 4] = kept_part.astype(jnp.bfloat16)
    pair = occ_ref[...].astype(F32)
    row8 = lax.broadcasted_iota(jnp.int32, (8, 128), 0)
    levels[occ] = jnp.where(row8 == 0, pair[:, 0:1], pair[:, 1:2])

    pl.semaphore_wait(barrier, jnp.where((z == 0) | (z == 3), 3, 4))

    def copy(zs, xs, cs, n, send_sem, to_occ, to_x):
        return pltpu.make_async_remote_copy(
            src_ref=blocks.at[zs, xs, cs, n],
            dst_ref=blocks.at[zs, xs, cs, n],
            send_sem=send_sem,
            recv_sem=recv.at[zs, xs, cs, n],
            device_id={"occ": to_occ, "aux": to_x},
            device_id_type=MESH,
        )

    def go_right(zs, n):
        return copy(zs, x, c, n, s_right.at[zs, n], right_id, x)

    def go_left(zs, n):
        return copy(zs, x, c, n, s_left.at[zs, n], left_id, x)

    def go_aux(zs, n):
        return copy(zs, x, c, n, s_aux.at[zs, n], occ, 1 - x)

    def go_core(zs, xs, n):
        return copy(zs, xs, c, n, s_core.at[zs, xs, n], core_id, x)

    def arrived(zs, xs, cs, n):
        copy(zs, xs, cs, n, s_right.at[0, 0], core_id, x).wait_recv()

    def among(n, pair_of):
        return (n == pair_of[0]) | (n == pair_of[1])

    def spread(zs, n):
        @pl.when(among(n, other))
        def _():
            go_aux(zs, n).start()

        @pl.when(among(n, own))
        def _():
            go_core(zs, x, n).start()

    def take_aux(zs):
        for m in range(2):
            arrived(zs, 1 - x, c, own[m])
            go_core(zs, 1 - x, own[m]).start()

    def send_right(zs, n):
        @pl.when((z < 3) & (n >= z))
        def _():
            go_right(zs, n).start()

    def send_left(zs, n):
        @pl.when((z > 0) & (n < left_lim))
        def _():
            go_left(zs, n).start()

    def level_copy(zs, cs, send_sem, to_occ):
        return pltpu.make_async_remote_copy(
            src_ref=levels.at[2 * zs + cs], dst_ref=levels.at[2 * zs + cs],
            send_sem=send_sem, recv_sem=r_lev.at[2 * zs + cs],
            device_id={"occ": to_occ, "aux": x}, device_id_type=MESH,
        )

    def level_right(zs):
        return level_copy(zs, c, s_lev.at[0, zs], right_id)

    def level_left(zs):
        return level_copy(zs, c, s_lev.at[1, zs], left_id)

    def level_core(zs):
        return level_copy(zs, c, s_lev.at[2, zs], core_id)

    def level_arrived(zs, cs):
        level_copy(zs, cs, s_lev.at[0, 0], core_id).wait_recv()

    def pass_levels(zs, right, left):
        if right:
            @pl.when(z < 3)
            def _():
                level_right(zs).start()
        if left:
            @pl.when(z > 0)
            def _():
                level_left(zs).start()
        level_core(zs).start()

    pass_levels(z, True, True)
    for n in range(4):
        send_right(z, 3 - n)

        @pl.when((z != 2) | (n < 2))
        def _():
            send_left(z, n)
    for n in range(4):
        spread(z, n)

    fetches[3].wait()
    fetches[4].wait()
    across = jnp.broadcast_to(vir_ref[...].astype(F32)[None], (256, 256))
    base[...] = across + across.T
    energy[...] = jnp.zeros_like(energy)

    def from_right(zs, n):
        arrived(zs, x, c, n)
        send_left(zs, n)
        spread(zs, n)

    for t in range(1, 4):
        @pl.when(z >= t)
        def _():
            level_arrived(jnp.maximum(z - t, 0), c)
            pass_levels(jnp.maximum(z - t, 0), True, False)

        @pl.when(z + t <= 3)
        def _():
            level_arrived(jnp.minimum(z + t, 3), c)
            pass_levels(jnp.minimum(z + t, 3), False, True)

        for step in range(4):
            @pl.when((z >= t) & (3 - step >= z - 1))
            def _():
                zs = jnp.maximum(z - t, 0)
                arrived(zs, x, c, 3 - step)
                send_right(zs, 3 - step)
                spread(zs, 3 - step)

            late = (z == 1) & (step >= 2)

            @pl.when((z + t <= 3) & (step < left_lim_in) & jnp.logical_not(late))
            def _():
                from_right(jnp.minimum(z + t, 3), step)
                if t == 1 and step == 1:
                    @pl.when(z == 2)
                    def _():
                        send_left(z, 2)
                        send_left(z, 3)

        if t == 2:
            @pl.when(z == 1)
            def _():
                for zs in (2, 3):
                    for n in (2, 3):
                        from_right(zs, n)

        if t == 1:
            take_aux(z)
        else:
            @pl.when(z >= t - 1)
            def _():
                take_aux(jnp.maximum(z - t + 1, 0))

            @pl.when(z + t - 1 <= 3)
            def _():
                take_aux(jnp.minimum(z + t - 1, 3))

    @pl.when(z >= 3)
    def _():
        take_aux(jnp.maximum(z - 3, 0))

    @pl.when(z + 3 <= 3)
    def _():
        take_aux(jnp.minimum(z + 3, 3))

    for zs in range(4):
        for xs in range(2):
            for m in range(2):
                arrived(zs, xs, 1 - c, own[m])

    diag = (x == 0) & ((z == 0) | (z == 3))
    for kk in range(4):
        @pl.when((diag & (kk // 2 == c)) | (jnp.logical_not(diag) & ((kk == c) | (kk >= 2))))
        def _():
            n = own[kk // 2]
            for o in range(2):
                for xs in range(2):
                    for zs in range(4):
                        for cs in range(2):
                            mat[pl.ds(zs * 128 + cs * 64, 64), pl.ds(xs * 128, 128)] = blocks[
                                zs, xs, cs, n, 2 * (kk % 2) + o]
                prod = lax.dot_general(
                    mat[...], metric_ref[...], (((0,), (0,)), ((), ())),
                    preferred_element_type=F32)
                fac[2 * kk + o] = prod.astype(jnp.bfloat16)

    for zs in range(4):
        level_arrived(zs, 1 - c)

    rows8 = lax.broadcasted_iota(jnp.int32, (8, 128), 0)
    lanes8 = lax.broadcasted_iota(jnp.int32, (8, 128), 1)

    def one_pair(t):
        li = jnp.where(diag, 4 * c + t % 4, 2 * c + t // 4)
        lj = jnp.where(diag, 4 * c + (t % 4 + t // 4) % 4, 4 + t % 4)
        gi = 4 * jnp.where(li < 4, own[0], own[1]) + li % 4
        gj = 4 * jnp.where(lj < 4, own[0], own[1]) + lj % 4
        fi, fj = fac[li], fac[lj]
        dims = (((1,), (1,)), ((), ()))
        direct = lax.dot_general(fi, fj, dims, preferred_element_type=F32)
        swapped = lax.dot_general(fj, fi, dims, preferred_element_type=F32)
        pair_level = levels[gi // 2, pl.ds(gi % 2, 1), :] + levels[gj // 2, pl.ds(gj % 2, 1), :]
        pair_level = jnp.concatenate([pair_level, pair_level], axis=1)
        term = direct * (2.0 * direct - swapped) / (base[...] - pair_level)
        term = -jnp.sum(jnp.sum(term, axis=0, keepdims=True), axis=1, keepdims=True)
        upper = (rows8 == gi % 2) & (lanes8 == gj % 8)
        energy[li // 2] += jnp.where(upper, term, 0.0)
        turned = (rows8 == gj % 2) & (lanes8 == gi % 8) & (gi != gj)
        energy[lj // 2] += jnp.where(turned, term, 0.0)

    def two_pairs(t, carry):
        one_pair(2 * t)
        one_pair(2 * t + 1)
        return carry

    lax.fori_loop(0, jnp.where(diag, 5, 4), two_pairs, 0)

    used = [jnp.logical_not(diag) | (c == h // 2) for h in range(4)]
    owner_occ = [2 * own[h // 2] + h % 2 for h in range(4)]
    column = [jnp.where(diag, own[h // 2], own[1 - h // 2]) for h in range(4)]
    slot = [column[h] % 2 * 2 + jnp.where(diag, 0, c) for h in range(4)]
    to_self = [(owner_occ[h] == occ) & (column[h] // 2 == x) for h in range(4)]

    def out_copy(h):
        return pltpu.make_async_remote_copy(
            src_ref=energy.at[h], dst_ref=shares.at[slot[h]],
            send_sem=s_out.at[h], recv_sem=r_out.at[slot[h]],
            device_id={"occ": owner_occ[h], "aux": column[h] // 2}, device_id_type=MESH,
        )

    for h in range(4):
        @pl.when(used[h] & jnp.logical_not(to_self[h]))
        def _():
            out_copy(h).start()

    for n in range(4):
        for t in range(4):
            @pl.when((z >= t) & (z < 3) & (n >= z))
            def _():
                go_right(jnp.maximum(z - t, 0), n).wait_send()

            @pl.when((z + t <= 3) & (z > 0) & (n < left_lim))
            def _():
                go_left(jnp.minimum(z + t, 3), n).wait_send()
    for zs in range(4):
        for m in range(2):
            go_aux(zs, other[m]).wait_send()
            for xs in range(2):
                go_core(zs, xs, own[m]).wait_send()
    for t in range(4):
        @pl.when((z >= t) & (z < 3))
        def _():
            level_right(jnp.maximum(z - t, 0)).wait_send()

        @pl.when((z + t <= 3) & (z > 0))
        def _():
            level_left(jnp.minimum(z + t, 3)).wait_send()

        level_core(t).wait_send()

    gathered[...] = jnp.zeros_like(gathered)
    for h in range(4):
        @pl.when(used[h] & to_self[h])
        def _():
            gathered[...] += energy[h]
    for kk in range(2):
        for cs in range(2):
            col = 2 * x + kk
            off_self = ((own[0] == z) & (own[1] == col)) | ((own[1] == z) & (own[0] == col))
            diag_self = (col == z) & (jnp.where(c == 0, own[0], own[1]) == z)
            mine = jnp.where(diag, diag_self, off_self & (cs == c))

            @pl.when(((col != z) | (cs == 0)) & jnp.logical_not(mine))
            def _():
                pltpu.make_async_remote_copy(
                    src_ref=energy.at[0], dst_ref=shares.at[2 * kk + cs],
                    send_sem=s_out.at[0], recv_sem=r_out.at[2 * kk + cs],
                    device_id={"occ": core_id}, device_id_type=MESH,
                ).wait_recv()
                gathered[...] += shares[2 * kk + cs]
    out_ref[...] = gathered[0:2, 0:8]
    for h in range(4):
        @pl.when(used[h] & jnp.logical_not(to_self[h]))
        def _():
            out_copy(h).wait_send()


def fused_body(raw_ints, kept, eps_occ, eps_vir, metric_factor):
    bf, dma = jnp.bfloat16, pltpu.SemaphoreType.DMA
    vmem = pl.BlockSpec(memory_space=pltpu.VMEM)
    return pl.pallas_call(
        kernel,
        out_shape=jax.ShapeDtypeStruct((2, 8), F32),
        in_specs=[pl.BlockSpec(memory_space=pl.ANY)] * 5,
        out_specs=vmem,
        scratch_shapes=[
            pltpu.VMEM((16, 64, 128), bf),
            pltpu.SMEM((4, 4, 8), jnp.int32),
            pltpu.VMEM((1, 2), bf),
            pltpu.VMEM((256,), bf),
            pltpu.VMEM((512, 512), bf),
            pltpu.VMEM((4, 2, 2, 4, 4, 64, 128), bf),
            pltpu.VMEM((512, 256), bf),
            pltpu.VMEM((8, 256, 512), bf),
            pltpu.VMEM((256, 256), F32),
            pltpu.VMEM((8, 8, 128), F32),
            pltpu.VMEM((4, 8, 128), F32),
            pltpu.VMEM((4, 8, 128), F32),
            pltpu.VMEM((8, 128), F32),
            dma((5,)),
            dma((4, 2, 2, 4)),
            dma((4, 4)),
            dma((4, 4)),
            dma((4, 4)),
            dma((4, 2, 4)),
            dma((3, 4)),
            dma((8,)),
            dma((4,)),
            dma((4,)),
        ],
        compiler_params=pltpu.CompilerParams(
            collective_id=0, has_side_effects=True, vmem_limit_bytes=60 * 2**20
        ),
    )(
        raw_ints.transpose(0, 2, 1), kept.transpose(1, 2, 0), eps_occ[None], eps_vir,
        metric_factor,
    )


def pair_terms(
    left_slice, right_all, left_cols, right_slice, own_levels, part_levels, vir_rows, vir_cols
):
    direct = jnp.einsum("iap,jbp->iajb", left_slice, right_all, preferred_element_type=jnp.float32)
    swapped = jnp.einsum(
        "ibp,jap->iajb", left_cols, right_slice, preferred_element_type=jnp.float32
    )
    own_f = own_levels.astype(jnp.float32)
    part_f = part_levels.astype(jnp.float32)
    rows_f = vir_rows.astype(jnp.float32)
    cols_f = vir_cols.astype(jnp.float32)
    denom = (
        rows_f[None, :, None, None]
        + cols_f[None, None, None, :]
        - own_f[:, None, None, None]
        - part_f[None, None, :, None]
    )
    return -jnp.sum(direct * (2.0 * direct - swapped) / denom, axis=(1, 3))


def body(raw_ints, kept, eps_occ, eps_vir, metric_factor):
    total_occ = raw_ints.shape[0]
    slice_vir = raw_ints.shape[1]
    slice_aux = raw_ints.shape[2]
    naux_all = metric_factor.shape[0]
    own_occ = eps_occ.shape[0]
    block_count = kept.shape[2]
    occ_index = lax.axis_index("occ")
    aux_index = lax.axis_index("aux")
    repeated = jnp.repeat(jnp.repeat(kept, total_occ // kept.shape[0], axis=0), VB, axis=1)
    kept_vir = lax.dynamic_slice_in_dim(repeated, aux_index * slice_vir, slice_vir, 1)
    aux_start = occ_index * slice_aux
    positions = aux_start + jnp.arange(slice_aux, dtype=jnp.int32)
    block_ids = positions // PB
    onehot = (block_ids[:, None] == jnp.arange(block_count, dtype=jnp.int32)[None, :]).astype(
        jnp.int32
    )
    kept_here = jnp.sum(kept_vir[:, :, None, :] * onehot[None, None, :, :], axis=3)
    offset = positions % PB
    screened = jnp.where(offset[None, None, :] < kept_here, raw_ints, jnp.zeros_like(raw_ints))
    relaid = lax.all_to_all(screened, "occ", split_axis=0, concat_axis=2, tiled=True)
    own_slice = jnp.dot(
        relaid.reshape(own_occ * slice_vir, naux_all),
        metric_factor,
        preferred_element_type=jnp.float32,
    )
    own_slice = own_slice.astype(jnp.bfloat16).reshape(own_occ, slice_vir, naux_all)
    vir_rows = lax.dynamic_slice_in_dim(eps_vir, aux_index * slice_vir, slice_vir)
    empty = jnp.zeros((own_occ, total_occ), jnp.float32)
    own_full = lax.all_gather(own_slice, "aux", axis=1, tiled=True)
    partner_rows = lax.all_gather(own_full, "occ", axis=0, tiled=True)
    partner_levels = lax.all_gather(eps_occ, "occ", axis=0, tiled=True)
    blocks_in = partner_rows.shape[0] // own_occ

    def add_block(block_no, totals):
        part_block = lax.dynamic_slice_in_dim(partner_rows, block_no * own_occ, own_occ, 0)
        part_level = lax.dynamic_slice_in_dim(partner_levels, block_no * own_occ, own_occ, 0)
        part_slice = lax.dynamic_slice_in_dim(part_block, aux_index * slice_vir, slice_vir, 1)
        term = pair_terms(
            own_slice, part_block, own_full, part_slice, eps_occ, part_level, vir_rows, eps_vir
        )
        column = block_no * own_occ
        before = lax.dynamic_slice_in_dim(totals, column, own_occ, 1)
        return lax.dynamic_update_slice_in_dim(totals, before + term, column, 1)

    energies = lax.fori_loop(0, blocks_in, add_block, empty)
    return lax.psum_scatter(energies, "aux", scatter_dimension=1, tiled=True)


def solution(mesh):
    in_specs = (
        P("parts", "aux", "occ"),
        P("parts", None, None),
        P(("parts", "occ")),
        P("parts"),
        P(),
    )
    out_specs = P(("parts", "occ"), "aux")
    fits = mesh.shape["occ"] == 8 and mesh.shape["aux"] == 2

    def step(raw_ints, kept, eps_occ, eps_vir, metric_factor):
        sizes = (raw_ints.shape, kept.shape, eps_occ.shape, eps_vir.shape)
        fused = fits and sizes == ((16, 128, 64), (8, 4, 4), (2,), (256,))
        run = fused_body if fused else body
        return run(raw_ints, kept, eps_occ, eps_vir, metric_factor)

    return jax.shard_map(step, mesh=mesh, in_specs=in_specs, out_specs=out_specs, check_vma=False)
```
